256 devices in a mesh: dp: 2 (over x_hi), expert: 2 (over core), ff: 32 (over z, y), mp: 2 (over x_lo).
Axes of the slice: x: 4 (x_hi: 2, x_lo: 2; x = x_hi * 2 + x_lo), y: 4, z: 8, core: 2. Of those that a mesh axis runs over, the one named last changes fastest.
Arguments:
- grad_tokens: bfloat16 [2, 1024, 3072], P('dp', ('expert', 'ff'), 'mp'), may hold values from -6 to 6
- routes: int32 [2, 1024, 2], P('dp', ('expert', 'ff')), may hold values from 0 to 1, all different within a row; in each aligned block of 16 rows (0 to 15, 16 to 31, ..., all dimensions but the last counted through in order) at most 16 rows name the same one
- gates: float32 [2, 1024, 2], P('dp', ('expert', 'ff')), may hold values from 0.1 to 1
- hidden_act: bfloat16 [2, 2, 1024, 8192], P('dp', 'expert', None, 'ff'), may hold values from -0.59765625 to 0.59765625
- weight: bfloat16 [2, 8192, 3072], P('expert', 'ff', 'mp'), may hold values from -0.0625 to 0.0625
Outputs:
- grad_hidden: bfloat16 [2, 2, 1024, 8192], P('dp', 'expert', 'mp', 'ff')
- grad_weight: float32 [2, 8192, 3072], P('expert', 'ff', ('mp', 'dp'))
The draws below stay inside these ranges and needn't reach their ends.
Inputs may be any that keep to these rules, and one draw needn't show every extreme that they name: The 16 tokens of one device send at most 16 routes to one expert, and some device sends exactly 16; a token's two experts differ.
All inputs are finite; a program needn't handle non-finite values.
Results may differ from the reference program's by a relative error of at most 0.011.
Values may be sent and summed in bfloat16 or wider, within the bound.
A program may use at most 64 MiB of HBM per device.

```python
import math
import jax
import jax.numpy as jnp
import numpy as np
from jax import lax

D = 3072
FF = 8192
TOK_DEV = 16
EXPERTS = 2
SLOT = 16
CAP = 1024
TOK_REP = 1024
N_DP = 2
N_EXPERT = 2
N_FF = 32
N_MP = 2


def steps_of(stream_key, dims, split, smallest, top_value):
    gain, own = 1.0, jax.random.fold_in(stream_key, 6)
    for dim, shards_of in split:
        heights = jnp.exp(jax.random.uniform(jax.random.fold_in(own, dim), (shards_of,), jnp.float32, smallest / len(split), top_value / len(split)))
        gain = gain * jnp.repeat(heights, dims[dim] // shards_of).reshape([-1 if axis == dim else 1 for axis in range(len(dims))])
    return gain


def assign_block(own_key, own, number, rows, amount, top, bound, slope):
    order = jax.random.permutation(own_key, amount)
    crowded, usual = load_shares(amount, rows * top, bound, slope, True), load_shares(amount, rows * top, bound, slope, False)
    places = jnp.arange(amount)

    def named(sizes, offset_by):
        used = int((sizes > 0).sum())
        fixed = max(1, used // 4)
        passed = fixed + (places - fixed + offset_by * (used - fixed)) % max(1, amount - fixed)
        return jnp.zeros((amount,), jnp.int32).at[order[jnp.where(places < fixed, places, passed)]].set(jnp.asarray(sizes, jnp.int32))

    sizes = jnp.where(number % 4 == 0, named(crowded, number // 4), named(usual, number - number // 4 - 1))
    mixed = jax.random.permutation(jax.random.fold_in(own, 3), amount)
    giver, sink = mixed[0:amount // 2 * 2:2], mixed[1:amount // 2 * 2:2]
    room = jnp.minimum(sizes[giver] - 1, bound - sizes[sink]) // 2
    room = jnp.where((giver == order[0]) | (sink == order[0]) | (sizes[sink] == 0), 0, jnp.maximum(room, 0))
    passed = jax.random.randint(jax.random.fold_in(own, 4), (amount // 2,), 0, 1 << 20) % (room + 1)
    sizes = sizes.at[giver].add(-passed).at[sink].add(passed)
    labels = jnp.searchsorted(jnp.cumsum(sizes), jnp.arange(rows * top), side="right").astype(jnp.int32)
    grid = labels.reshape(top, rows).T
    grid = grid[jax.random.permutation(jax.random.fold_in(own, 1), rows)]
    offset_by = jax.random.randint(jax.random.fold_in(own, 2), (rows, 1), 0, top)
    return jnp.take_along_axis(grid, (jnp.arange(top)[None, :] + offset_by) % top, axis=1)


def load_shares(number_of, total, bound, skew, full):
    weights = [(1 << 20) // math.isqrt(standing ** skew) + 1 for standing in range(1, number_of + 1)]
    largest = bound if full else min(bound, max(-(-total // number_of), total * weights[0] // sum(weights)))
    least = 1 if total - largest >= number_of - 1 else 0
    given, rest = [largest] + [least] * (number_of - 1), total - largest - least * (number_of - 1)
    while rest > 0:
        movable = [i for i in range(1, number_of) if given[i] < largest] or [i for i in range(1, number_of) if given[i] < bound]
        mass, left = sum([weights[i] for i in movable]), rest
        for i in movable:
            addition = min(bound - given[i], max(1, left * weights[i] // mass), rest)
            given[i] = given[i] + addition
            rest = rest - addition
    return np.array(given)


def gaussian(rng, shape, spread, limit, pieces=(), kind=jnp.bfloat16):
    result = spread * jax.random.normal(rng, shape, jnp.float32)
    if pieces:
        result = result * steps_of(rng, shape, pieces, -0.22, 0.18)
    return jnp.clip(result, -limit, limit).astype(kind)


def setup_inputs(seed: int = 0) -> dict:
    splits = jax.random.split(jax.random.key(seed), 6)
    grad_tokens = gaussian(splits[0], (N_DP, TOK_REP, D), 1.0, 6.0, ((0, 2), (1, 64), (2, 2)))
    routes_keys = jax.random.split(jax.random.fold_in(splits[1], 1), N_DP * TOK_REP // TOK_DEV)
    routes_turns = jax.random.permutation(jax.random.fold_in(splits[1], 3), N_DP * TOK_REP // TOK_DEV)
    routes = jax.vmap(lambda own, number: assign_block(jax.random.fold_in(splits[1], 2), own, number, TOK_DEV, EXPERTS, 2, SLOT, 2))(routes_keys, routes_turns).reshape((N_DP, TOK_REP, 2))
    gates = jnp.clip(0.1 + 0.9 * jax.random.uniform(splits[2], (N_DP, TOK_REP, 2), jnp.float32) ** steps_of(splits[2], (N_DP, TOK_REP, 2), ((0, 2), (1, 64)), -0.2, 0.2), 0.1, 1.0)
    hidden_act = gaussian(splits[3], (N_DP, EXPERTS, CAP, FF), 0.1, 0.59765625, ((0, 2), (1, 2), (3, 32)))
    weight = gaussian(splits[4], (EXPERTS, FF, D), FF ** -0.5, 0.0625, ((0, 2), (1, 32), (2, 2)))
    return {"grad_tokens": grad_tokens, "routes": routes, "gates": gates, "hidden_act": hidden_act, "weight": weight}


def dispatch(grad_rep, route_rep, gate_rep):
    sources = N_EXPERT * N_FF
    route_ids = route_rep.reshape(sources, TOK_DEV * 2).astype(jnp.int32)
    expert_ids = jnp.arange(EXPERTS, dtype=jnp.int32)
    one_hot = (route_ids[:, :, None] == expert_ids[None, None, :]).astype(jnp.int32)
    slot_index = jnp.sum((jnp.cumsum(one_hot, axis=1) - 1) * one_hot, axis=2)
    position = (jnp.arange(sources, dtype=jnp.int32)[:, None] * SLOT + slot_index).astype(jnp.int32)
    scaled = (grad_rep[:, None, :].astype(jnp.float32) * gate_rep[:, :, None]).astype(jnp.bfloat16)
    scaled = scaled.reshape(sources * TOK_DEV * 2, D)
    empty = jnp.zeros((EXPERTS, CAP, D), jnp.bfloat16)
    return empty.at[route_ids.reshape(-1), position.reshape(-1)].set(scaled)


def reference(grad_tokens, routes, gates, hidden_act, weight):
    width = D // N_MP
    routed = jnp.stack([dispatch(grad_tokens[r], routes[r], gates[r]) for r in range(N_DP)])

    def per_expert(packed):
        rows_e, saved_e, weight_e = packed
        hidden_list = []
        grad_w = jnp.zeros((FF, D), jnp.float32)
        for r in range(N_DP):
            total = jnp.zeros((CAP, FF), jnp.float32)
            for j in range(N_MP):
                part_grad = jnp.dot(rows_e[r][:, j * width:(j + 1) * width], weight_e[:, j * width:(j + 1) * width].T, preferred_element_type=jnp.float32)
                total = total + lax.optimization_barrier(part_grad.astype(jnp.bfloat16)).astype(jnp.float32)
            hidden_list.append(total.astype(jnp.bfloat16))
            grad_w = grad_w + lax.dot_general(saved_e[r], rows_e[r], (((0,), (0,)), ((), ())), preferred_element_type=jnp.float32)
        return jnp.stack(hidden_list), grad_w

    grad_hidden, grad_weight = lax.map(per_expert, (jnp.swapaxes(routed, 0, 1), jnp.swapaxes(hidden_act, 0, 1), weight))
    return jnp.swapaxes(grad_hidden, 0, 1), grad_weight
```

```python
import jax
import jax.numpy as jnp
from jax import lax
from jax.experimental import pallas as pl
from jax.experimental.pallas import tpu as pltpu
from jax.sharding import PartitionSpec as P

MESH = pl.DeviceIdType.MESH
NY, NZ = 4, 8
GATE = 128
FIRST = 640
YS = (1, 3, 2)
NEAR = (2, -2, 1, -1)
PAIRS = ((0, 1), (-1, 2), (-2, 3), (-3, 4))
DIST = (0, 1, -1, 2, -2, 3, -3, 4)


def kernel(tok_hbm, gate_ref, route_ref, hid_hbm, w_hbm, gh_ref, keep_hbm, got_hbm,
           rows, hid, w, acc_s, acc_k, gh_keep, gh_send, gh_got, gw_send, gw_got, in_sem, out_sem, send_sem, recv_sem):
    dp, e, f, mp = (lax.axis_index(a) for a in ("dp", "expert", "ff", "mp"))
    y, z = lax.rem(f, NY), f // NY
    width = w.shape[1]
    half = width // 2

    def dev(dy=0, dz=0):
        return (dp, e, lax.rem(z + dz + NZ, NZ) * NY + lax.rem(y + dy + NY, NY), mp)

    def plane(d):
        return lax.rem(z + d + NZ, NZ)

    sibling, across, pair = (dp, 1 - e, f, mp), (1 - dp, e, f, mp), (dp, e, f, 1 - mp)
    loads = [
        pltpu.make_async_copy(tok_hbm, rows.at[e, z, y, :, pl.ds(0, width)], in_sem.at[0]),
        pltpu.make_async_copy(hid_hbm, hid, in_sem.at[1]),
        pltpu.make_async_copy(w_hbm, w, in_sem.at[2]),
    ]
    loads[0].start()
    barrier = pltpu.get_barrier_semaphore()
    partners = [dev(dy=k) for k in YS] + [dev(dz=d) for d in NEAR] + [sibling, across, pair]
    for p in partners:
        pl.semaphore_signal(barrier, inc=1, device_id=p, device_id_type=MESH)
    for load in loads[1:]:
        load.start()

    tok = rows.shape[3]
    diag = lax.broadcasted_iota(jnp.int32, (tok, tok), 0) == lax.broadcasted_iota(jnp.int32, (tok, tok), 1)
    lane = lax.broadcasted_iota(jnp.int32, (tok, GATE), 1)
    block = jnp.zeros((tok, GATE), jnp.float32)
    for expert in range(2):
        mine = jnp.sum(jnp.where(route_ref[...] == expert, gate_ref[...], 0.0), axis=0, keepdims=True)
        col = jnp.sum(jnp.where(diag, jnp.broadcast_to(mine, (tok, tok)), 0.0), axis=1, keepdims=True)
        high = col.astype(jnp.bfloat16).astype(jnp.float32)
        block = jnp.where(lane == 2 * expert, high, jnp.where(lane == 2 * expert + 1, col - high, block))
    rows[e, z, y, :, pl.ds(width, GATE)] = block.astype(jnp.bfloat16)
    acc_s[...] = jnp.zeros_like(acc_s)
    acc_k[...] = jnp.zeros_like(acc_k)
    loads[0].wait()
    pl.semaphore_wait(barrier, len(partners))

    sent, count = [], [0]

    def send(src, dst, to):
        i = count[0]
        count[0] += 1
        copy = pltpu.make_async_remote_copy(
            src_ref=src, dst_ref=dst, send_sem=send_sem.at[i], recv_sem=recv_sem.at[i], device_id=to, device_id_type=MESH
        )
        copy.start()
        sent.append(copy)
        return copy

    part_a, part_b = pl.ds(0, FIRST), pl.ds(FIRST, width + GATE - FIRST)

    def a_plane(d, dz):
        ref = rows.at[e, plane(d), :, :, part_a]
        return send(ref, ref, dev(dz=dz))

    def b_block(d, dy=0, dz=0):
        ref = rows.at[e, plane(d), y, :, part_b]
        return send(ref, ref, dev(dy=dy, dz=dz))

    a_own = rows.at[e, z, y, :, part_a]
    a_y = [send(a_own, a_own, dev(dy=k)) for k in YS]
    b_z = {-dz: b_block(0, dz=dz) for dz in NEAR}
    b_y = {0: [b_block(0, dy=k) for k in YS]}
    for copy in a_y:
        copy.wait_recv()
    a_z = {-dz: a_plane(0, dz) for dz in NEAR}
    b_z[-2].wait_recv()
    b_z[-3] = b_block(-2, dz=1)
    b_y[-2] = [b_block(-2, dy=k) for k in YS]
    b_z[2].wait_recv()
    b_z[3] = b_block(2, dz=-1)
    b_z[4] = b_block(2, dz=-2)
    b_y[2] = [b_block(2, dy=k) for k in YS]
    for d in (-1, 1):
        b_z[d].wait_recv()
        b_y[d] = [b_block(d, dy=k) for k in YS]
    a_z[-2].wait_recv()
    a_z[-3] = a_plane(-2, 1)
    a_z[4] = a_plane(-2, 2)
    a_z[2].wait_recv()
    a_z[3] = a_plane(2, -1)
    for d in (-3, 3, 4):
        b_z[d].wait_recv()
        b_y[d] = [b_block(d, dy=k) for k in YS]

    halves = {}

    def finish(d):
        if d in (1, -1, 3, -3, 4):
            a_z[d].wait_recv()
        for copy in b_y[d]:
            copy.wait_recv()
        ref = rows.at[e, plane(d)]
        halves[d] = send(ref, ref, sibling)

    off_s = pl.multiple_of((1 - dp) * half, half)
    off_k = pl.multiple_of(dp * half, half)
    gh_sends, gw_sends = [], []
    n_rows = NY * tok
    step = 256

    def compute(ds, last):
        places = [(c, plane(d)) for c in (mp, 1 - mp) for d in ds]

        def take(at):
            return jnp.concatenate([rows[c, p, :, :, at].reshape(n_rows, -1) for c, p in places], axis=0)

        gates = take(pl.ds(width, GATE)).astype(jnp.float32)
        lanes = lax.broadcasted_iota(jnp.int32, gates.shape, 1)
        g = jnp.sum(jnp.where((lanes // 2) == e, gates, 0.0), axis=1, keepdims=True)
        h = jnp.concatenate([hid[c, p] for c, p in places], axis=0)
        h = (h.astype(jnp.float32) * g).astype(jnp.bfloat16)

        def grow(acc, off, n):
            x = take(pl.ds(pl.multiple_of(off + n, 128), step))
            return acc[:, n:n + step] + lax.dot_general(h, x, (((0,), (0,)), ((), ())), preferred_element_type=jnp.float32)

        for i, n in enumerate(range(0, half, step)):
            total = grow(acc_s, off_s, n)
            if last:
                gw_send[i] = total.astype(jnp.bfloat16)
                gw_sends.append(send(gw_send.at[i], gw_got.at[i], across))
            else:
                acc_s[:, n:n + step] = total
        gh = lax.dot_general(take(pl.ds(0, width)), w[...], (((1,), (1,)), ((), ())), preferred_element_type=jnp.float32) * g
        for i, d in enumerate(ds):
            gh_keep[plane(d)] = gh[i * n_rows:(i + 1) * n_rows]
            j = i + len(ds)
            gh_send[plane(d)] = gh[j * n_rows:(j + 1) * n_rows].astype(jnp.bfloat16)
            gh_sends.append(send(gh_send.at[plane(d)], gh_got.at[plane(d)], pair))
        for n in range(0, half, step):
            acc_k[:, n:n + step] = grow(acc_k, off_k, n)

    finish(0)
    loads[1].wait()
    loads[2].wait()
    finish(1)
    finish(-1)
    finish(2)
    for i, ds in enumerate(PAIRS):
        for d in ds:
            halves[d].wait_recv()
        compute(ds, i == len(PAIRS) - 1)
        if i == 0:
            finish(-2)
            finish(3)
        if i == 1:
            finish(-3)
            finish(4)

    keep_out = pltpu.make_async_copy(acc_k, keep_hbm, out_sem.at[0])
    keep_out.start()
    for copy in gh_sends:
        copy.wait_recv()
    gh_ref[...] = (gh_keep[...] + gh_got[...].astype(jnp.float32)).astype(jnp.bfloat16)
    keep_out.wait()
    for copy in sent:
        copy.wait_send()
    outs = []
    for i, copy in enumerate(gw_sends):
        copy.wait_recv()
        out = pltpu.make_async_copy(gw_got.at[i], got_hbm.at[i], out_sem.at[i + 1])
        out.start()
        outs.append(out)
    for out in outs:
        out.wait()


def body(grad_tokens, routes, gates, hidden_act, weight):
    _, tok, width = grad_tokens.shape
    cap, ff = hidden_act.shape[2:]
    half, n_rows = width // 2, NY * tok
    pieces = half // 256
    n_copies = 3 + 4 + 3 + 7 + 3 * NZ + NZ + NZ + pieces
    vmem, hbm = pl.BlockSpec(memory_space=pltpu.VMEM), pl.BlockSpec(memory_space=pl.ANY)
    bf16, f32 = jnp.bfloat16, jnp.float32
    gh, keep, got = pl.pallas_call(
        kernel,
        out_shape=(
            jax.ShapeDtypeStruct((NZ, n_rows, ff), bf16),
            jax.ShapeDtypeStruct((ff, half), f32),
            jax.ShapeDtypeStruct((pieces, ff, 256), bf16),
        ),
        in_specs=[hbm, vmem, vmem, hbm, hbm],
        out_specs=(vmem, hbm, hbm),
        scratch_shapes=[
            pltpu.VMEM((2, NZ, NY, tok, width + GATE), bf16),
            pltpu.VMEM((2, NZ, n_rows, ff), bf16),
            pltpu.VMEM((ff, width), bf16),
            pltpu.VMEM((ff, half), f32),
            pltpu.VMEM((ff, half), f32),
            pltpu.VMEM((NZ, n_rows, ff), f32),
            pltpu.VMEM((NZ, n_rows, ff), bf16),
            pltpu.VMEM((NZ, n_rows, ff), bf16),
            pltpu.VMEM((pieces, ff, 256), bf16),
            pltpu.VMEM((pieces, ff, 256), bf16),
            pltpu.SemaphoreType.DMA((3,)),
            pltpu.SemaphoreType.DMA((1 + pieces,)),
            pltpu.SemaphoreType.DMA((n_copies,)),
            pltpu.SemaphoreType.DMA((n_copies,)),
        ],
        compiler_params=pltpu.CompilerParams(collective_id=0, has_side_effects=True, vmem_limit_bytes=32 * 2**20),
    )(
        grad_tokens[0],
        gates[0].T,
        routes[0].T,
        hidden_act.reshape(2, NZ, n_rows, ff),
        weight[0],
    )
    grad_hidden = gh.reshape(1, 1, cap // 2, ff)
    got = jnp.concatenate([got[i] for i in range(pieces)], axis=1)
    grad_weight = keep + got.astype(f32)
    return grad_hidden, grad_weight.reshape(1, ff, half)


def solution(mesh):
    in_specs = (
        P("dp", ("expert", "ff"), "mp"),
        P("dp", ("expert", "ff"), None),
        P("dp", ("expert", "ff"), None),
        P("dp", "expert", None, "ff"),
        P("expert", "ff", "mp"),
    )
    out_specs = (P("dp", "expert", "mp", "ff"), P("expert", "ff", ("mp", "dp")))
    return jax.shard_map(body, mesh=mesh, in_specs=in_specs, out_specs=out_specs, check_vma=False)
```

```python
import jax
import jax.numpy as jnp
from jax import lax
from jax.experimental import pallas as pl
from jax.experimental.pallas import tpu as pltpu
from jax.sharding import PartitionSpec as P

MESH = pl.DeviceIdType.MESH
NY, NZ = 4, 8
GATE = 128
SPLITS = (384, 256)
YS = (1, 3, 2)
NEAR = (2, -2, 1, -1)
PAIRS = ((0, 1), (-1, 2), (-2, 3), (-3, 4))
STEP = 256
N_COPIES = 2 * (3 + 4 + 3 + 7 + 3 * NZ + 2 * NZ) + NZ + 8


def kernel(tok_hbm, gate_hbm, route_hbm, hid_hbm, w_hbm, acc_k, gw_got, gh_keep, gh_got,
           gate_ref, route_ref, rows, hid, scaled, w, acc_s, gh_send, gw_send, in_sem, send_sem, recv_sem):
    dp, e, f, mp = (lax.axis_index(a) for a in ("dp", "expert", "ff", "mp"))
    y, z = lax.rem(f, NY), f // NY
    width = w.shape[1]
    half = width // 2

    def dev(dy=0, dz=0):
        return (dp, e, lax.rem(z + dz + NZ, NZ) * NY + lax.rem(y + dy + NY, NY), mp)

    def plane(d):
        return lax.rem(z + d + NZ, NZ)

    sibling, across, pair = (dp, 1 - e, f, mp), (1 - dp, e, f, mp), (dp, e, f, 1 - mp)

    off_s, off_k = pl.multiple_of((1 - dp) * half, half), pl.multiple_of(dp * half, half)
    at_s, at_k = pl.ds(GATE, half), pl.ds(GATE + half, half)
    own = rows.at[e, z, y]
    loads = [
        pltpu.make_async_copy(tok_hbm.at[:, pl.ds(off_s, half)], own.at[:, at_s], in_sem.at[0]),
        pltpu.make_async_copy(tok_hbm.at[:, pl.ds(off_k, half)], own.at[:, at_k], in_sem.at[1]),
        pltpu.make_async_copy(gate_hbm, gate_ref, in_sem.at[2]),
        pltpu.make_async_copy(route_hbm, route_ref, in_sem.at[3]),
    ]
    later = [
        pltpu.make_async_copy(hid_hbm, hid, in_sem.at[4]),
        pltpu.make_async_copy(w_hbm.at[:, pl.ds(off_s, half)], w.at[:, pl.ds(0, half)], in_sem.at[5]),
        pltpu.make_async_copy(w_hbm.at[:, pl.ds(off_k, half)], w.at[:, pl.ds(half, half)], in_sem.at[6]),
    ]
    for load in loads:
        load.start()
    barrier = pltpu.get_barrier_semaphore()
    partners = [dev(dy=k) for k in YS] + [dev(dz=d) for d in NEAR] + [sibling, across, pair]
    for p in partners:
        pl.semaphore_signal(barrier, inc=1, device_id=p, device_id_type=MESH)
    for load in later:
        load.start()
    acc_s[...] = jnp.zeros_like(acc_s)
    acc_k[...] = jnp.zeros_like(acc_k)

    tok = rows.shape[3]
    diag = lax.broadcasted_iota(jnp.int32, (tok, tok), 0) == lax.broadcasted_iota(jnp.int32, (tok, tok), 1)
    lane = lax.broadcasted_iota(jnp.int32, (tok, GATE), 1)
    block = jnp.zeros((tok, GATE), jnp.float32)
    loads[2].wait()
    loads[3].wait()
    for expert in range(2):
        mine = jnp.sum(jnp.where(route_ref[...] == expert, gate_ref[...], 0.0), axis=0, keepdims=True)
        col = jnp.sum(jnp.where(diag, jnp.broadcast_to(mine, (tok, tok)), 0.0), axis=1, keepdims=True)
        high = col.astype(jnp.bfloat16).astype(jnp.float32)
        block = jnp.where(lane == 2 * expert, high, jnp.where(lane == 2 * expert + 1, col - high, block))
    rows[e, z, y, :, pl.ds(0, GATE)] = block.astype(jnp.bfloat16)
    loads[0].wait()
    loads[1].wait()
    pl.semaphore_wait(barrier, len(partners))

    sent = []

    def send(src, dst, to):
        i = len(sent)
        copy = pltpu.make_async_remote_copy(
            src_ref=src, dst_ref=dst, send_sem=send_sem.at[i], recv_sem=recv_sem.at[i], device_id=to, device_id_type=MESH
        )
        copy.start()
        sent.append(copy)
        return copy

    def wait(copies):
        for copy in copies:
            copy.wait_recv()

    class Gather:
        def __init__(self, start, size, first):
            self.a, self.b = pl.ds(start, first), pl.ds(start + first, size - first)
            self.sib = {}

        def a_plane(self, d, dz):
            ref = rows.at[e, plane(d), :, :, self.a]
            return send(ref, ref, dev(dz=dz))

        def b_block(self, d, dy=0, dz=0):
            ref = rows.at[e, plane(d), y, :, self.b]
            return send(ref, ref, dev(dy=dy, dz=dz))

        def spread(self, d):
            self.b_y[d] = [self.b_block(d, dy=k) for k in YS]

        def start(self):
            ref = rows.at[e, z, y, :, self.a]
            self.a_y = [send(ref, ref, dev(dy=k)) for k in YS]
            self.b_z = {-dz: self.b_block(0, dz=dz) for dz in NEAR}
            self.b_y = {}
            self.spread(0)

        def a_near(self):
            wait(self.a_y)
            self.a_z = {-dz: self.a_plane(0, dz) for dz in NEAR}

        def b_far(self):
            self.b_z[-2].wait_recv()
            self.b_z[-3] = self.b_block(-2, dz=1)
            self.spread(-2)
            self.b_z[2].wait_recv()
            self.b_z[3] = self.b_block(2, dz=-1)
            self.b_z[4] = self.b_block(2, dz=-2)
            self.spread(2)
            for d in (-1, 1):
                self.b_z[d].wait_recv()
                self.spread(d)

        def a_far(self):
            self.a_z[-2].wait_recv()
            self.a_z[-3] = self.a_plane(-2, 1)
            self.a_z[4] = self.a_plane(-2, 2)
            self.a_z[2].wait_recv()
            self.a_z[3] = self.a_plane(2, -1)

        def b_last(self):
            for d in (-3, 3, 4):
                self.b_z[d].wait_recv()
                self.spread(d)

        def share_a(self, ds):
            for d in ds:
                if d not in (0, 2, -2):
                    self.a_z[d].wait_recv()
                ref = rows.at[e, plane(d), :, :, self.a]
                self.sib.setdefault(d, []).append(send(ref, ref, sibling))

        def share_b(self, ds):
            for d in ds:
                wait(self.b_y[d])
                ref = rows.at[e, plane(d), :, :, self.b]
                self.sib.setdefault(d, []).append(send(ref, ref, sibling))

    n_rows = NY * tok
    gh_sends, gw_sends = [], []

    def take(ds, at):
        parts = [rows[c, plane(d), :, :, at].reshape(n_rows, -1) for c in (mp, 1 - mp) for d in ds]
        return jnp.concatenate(parts, axis=0)

    def gate_of(ds):
        gates = take(ds, pl.ds(0, GATE)).astype(jnp.float32)
        lanes = lax.broadcasted_iota(jnp.int32, gates.shape, 1)
        return jnp.sum(jnp.where((lanes // 2) == e, gates, 0.0), axis=1, keepdims=True)

    def grow(i, ds, acc, start, n):
        x = take(ds, pl.ds(start + n, STEP))
        more = lax.dot_general(scaled[i], x, (((0,), (0,)), ((), ())), preferred_element_type=jnp.float32)
        return acc[:, n:n + STEP] + more

    def compute_s(i):
        ds = PAIRS[i]
        for d in ds:
            wait(first.sib[d])
        h = jnp.concatenate([hid[c, plane(d)] for c in (mp, 1 - mp) for d in ds], axis=0)
        scaled[i] = (h.astype(jnp.float32) * gate_of(ds)).astype(jnp.bfloat16)
        for n in range(0, half, STEP):
            total = grow(i, ds, acc_s, GATE, n)
            if i == len(PAIRS) - 1:
                at = pl.ds(n, STEP)
                gw_send[:, n:n + STEP] = total.astype(jnp.bfloat16)
                gw_sends.append(send(gw_send.at[:, at], gw_got.at[:, at], across))
            else:
                acc_s[:, n:n + STEP] = total

    def compute_k(i):
        ds = PAIRS[i]
        for d in ds:
            wait(second.sib[d])
        x = take(ds, pl.ds(GATE, width))
        gh = lax.dot_general(x, w[...], (((1,), (1,)), ((), ())), preferred_element_type=jnp.float32) * gate_of(ds)
        for j, d in enumerate(ds):
            gh_send[plane(d)] = gh[(j + 2) * n_rows:(j + 3) * n_rows].astype(jnp.bfloat16)
            gh_sends.append(send(gh_send.at[plane(d)], gh_got.at[plane(d)], pair))
            gh_keep[plane(d)] = gh[j * n_rows:(j + 1) * n_rows]
        for n in range(0, half, STEP):
            acc_k[:, n:n + STEP] = grow(i, ds, acc_k, GATE + half, n)

    first, second = Gather(0, GATE + half, SPLITS[0]), Gather(GATE + half, half, SPLITS[1])
    first.start()
    first.a_near()
    first.b_far()
    second.start()
    first.share_a((0,))
    first.share_b((0,))
    first.a_far()
    first.b_last()
    first.share_a((-2, 2, -1, 1))
    first.share_b((-2, 2, -1, 1))
    second.a_near()
    second.b_far()
    later[0].wait()
    compute_s(0)
    compute_s(1)
    second.share_a((0,))
    second.share_b((0,))
    first.share_a((-3, 3, 4))
    first.share_b((-3, 3, 4))
    second.a_far()
    second.b_last()
    second.share_a((-2, 2, -1, 1))
    second.share_b((-2, 2, -1, 1))
    compute_s(2)
    compute_s(3)
    later[1].wait()
    later[2].wait()
    compute_k(0)
    compute_k(1)
    second.share_a((-3, 3, 4))
    second.share_b((-3, 3, 4))
    compute_k(2)
    compute_k(3)
    for copy in sent:
        copy.wait_send()
    wait(gh_sends)
    wait(gw_sends)


def finish(acc_k, gw_got, gh_keep, gh_got, gh_hbm, gw_hbm, gh, gw, sem):
    gh[...] = (gh_keep[...] + gh_got[...].astype(jnp.float32)).astype(jnp.bfloat16)
    outs = [pltpu.make_async_copy(gh, gh_hbm, sem.at[0])]
    outs[0].start()
    n = gw.shape[0] // 4
    for i in range(4):
        at = pl.ds(i * n, n)
        gw[at] = acc_k[at] + gw_got[at].astype(jnp.float32)
        outs.append(pltpu.make_async_copy(gw.at[at], gw_hbm.at[at], sem.at[i + 1]))
        outs[-1].start()
    for out in outs:
        out.wait()


def body(grad_tokens, routes, gates, hidden_act, weight):
    _, tok, width = grad_tokens.shape
    cap, ff = hidden_act.shape[2:]
    half, n_rows = width // 2, NY * tok
    vmem, hbm = pl.BlockSpec(memory_space=pltpu.VMEM), pl.BlockSpec(memory_space=pltpu.HBM)
    bf16, f32 = jnp.bfloat16, jnp.float32
    operands = (
        grad_tokens[0],
        gates[0].T,
        routes[0].T,
        hidden_act.reshape(2, NZ, n_rows, ff),
        weight[0],
    )
    halves = pl.pallas_call(
        kernel,
        out_shape=(
            pltpu.VMEM((ff, half), f32),
            pltpu.VMEM((ff, half), bf16),
            pltpu.VMEM((NZ, n_rows, ff), f32),
            pltpu.VMEM((NZ, n_rows, ff), bf16),
        ),
        in_specs=[hbm] * 5,
        out_specs=(vmem,) * 4,
        scratch_shapes=[
            pltpu.VMEM((2, tok), f32),
            pltpu.VMEM((2, tok), jnp.int32),
            pltpu.VMEM((2, NZ, NY, tok, GATE + width), bf16),
            pltpu.VMEM((2, NZ, n_rows, ff), bf16),
            pltpu.VMEM((len(PAIRS), 4 * n_rows, ff), bf16),
            pltpu.VMEM((ff, width), bf16),
            pltpu.VMEM((ff, half), f32),
            pltpu.VMEM((NZ, n_rows, ff), bf16),
            pltpu.VMEM((ff, half), bf16),
            pltpu.SemaphoreType.DMA((7,)),
            pltpu.SemaphoreType.DMA((N_COPIES,)),
            pltpu.SemaphoreType.DMA((N_COPIES,)),
        ],
        compiler_params=pltpu.CompilerParams(collective_id=0, has_side_effects=True, vmem_limit_bytes=32 * 2**20),
    )(*(pltpu.with_memory_space_constraint(x, pltpu.HBM) for x in operands))
    gh, gw = pl.pallas_call(
        finish,
        out_shape=(jax.ShapeDtypeStruct((NZ, n_rows, ff), bf16), jax.ShapeDtypeStruct((ff, half), f32)),
        in_specs=[vmem] * 4,
        out_specs=(hbm, hbm),
        scratch_shapes=[
            pltpu.VMEM((NZ, n_rows, ff), bf16),
            pltpu.VMEM((ff, half), f32),
            pltpu.SemaphoreType.DMA((5,)),
        ],
        compiler_params=pltpu.CompilerParams(vmem_limit_bytes=16 * 2**20),
    )(*halves)
    return gh.reshape(1, 1, cap // 2, ff), gw.reshape(1, ff, half)


def solution(mesh):
    in_specs = (
        P("dp", ("expert", "ff"), "mp"),
        P("dp", ("expert", "ff"), None),
        P("dp", ("expert", "ff"), None),
        P("dp", "expert", None, "ff"),
        P("expert", "ff", "mp"),
    )
    out_specs = (P("dp", "expert", "mp", "ff"), P("expert", "ff", ("mp", "dp")))
    return jax.shard_map(body, mesh=mesh, in_specs=in_specs, out_specs=out_specs, check_vma=False)
```

```python
import functools

import jax
import jax.numpy as jnp
from jax import lax
from jax.experimental import pallas as pl
from jax.experimental.pallas import tpu as pltpu
from jax.sharding import PartitionSpec as P

MESH = pl.DeviceIdType.MESH
NY, NZ = 4, 8
GATE = 128
SPLITS = (256, 256)
YS = (1, 3, 2)
NEAR = (2, -2, 1, -1)
ALL = (2, -2, 1, -1, 3, -3, 4)
REACH = ((ALL, ALL), (ALL, NEAR))
PAIRS = ((0, 1), (-1, 2), (-2, 3), (-3, 4))
STEP = 256
N_COPIES = 2 * (3 + 7 + 7 + 3 * NZ + 2 * NZ) + NZ + 3


ORDERS = ((
    ("start", 0),
    ("a_near", 0),
    ("b_near", 0),
    ("share", 0, (0,)),
    ("start", 1),
    ("share", 0, (-2, 2, -1, 1)),
    ("share", 0, (-3, 3, 4)),
    ("a_near", 1),
    ("b_near", 1),
    ("receive", 0, PAIRS[0]),
    ("s", 0),
    ("receive", 0, PAIRS[1]),
    ("s", 1),
    ("receive", 0, PAIRS[2]),
    ("s", 2),
    ("receive", 0, PAIRS[3]),
    ("s", 3),
    ("share", 1, (0,)),
    ("share", 1, (-2, 2, -1, 1)),
    ("receive", 1, PAIRS[0]),
    ("k", 0),
    ("receive", 1, PAIRS[1]),
    ("k", 1),
    ("share", 1, (-3, 3, 4)),
    ("receive", 1, PAIRS[2]),
    ("k", 2),
    ("receive", 1, PAIRS[3]),
    ("k", 3),
), (
    ("start", 0),
    ("a_near", 0),
    ("b_near", 0),
    ("share", 0, (0,)),
    ("start", 1),
    ("share", 0, (-2, 2, -1, 1)),
    ("share", 0, (-3, 3, 4)),
    ("a_near", 1),
    ("b_near", 1),
    ("receive", 0, PAIRS[0]),
    ("s", 0),
    ("receive", 0, PAIRS[1]),
    ("s", 1),
    ("receive", 0, PAIRS[2]),
    ("s", 2),
    ("receive", 0, PAIRS[3]),
    ("s", 3),
    ("a_far", 1),
    ("b_far", 1),
    ("share", 1, (0,)),
    ("share", 1, (-2, 2, -1, 1)),
    ("receive", 1, PAIRS[0]),
    ("k", 0),
    ("receive", 1, PAIRS[1]),
    ("k", 1),
    ("share", 1, (-3, 3, 4)),
    ("receive", 1, PAIRS[2]),
    ("k", 2),
    ("receive", 1, PAIRS[3]),
    ("k", 3),
))


def kernel(tok_hbm, gate_hbm, route_hbm, hid_hbm, w_hbm, acc_k, gw_got, gh_keep, gh_got,
           gate_ref, route_ref, rows, hid, scaled, w, acc_s, gh_send, gw_send, in_sem, send_sem, recv_sem):
    dp, e, f, mp = (lax.axis_index(a) for a in ("dp", "expert", "ff", "mp"))
    y, z = f & (NY - 1), f // NY
    ys, zs = [(y + k) & (NY - 1) for k in range(NY)], [(z + k) & (NZ - 1) for k in range(NZ)]
    width = w.shape[1]
    half = width // 2

    def dev(dy=0, dz=0):
        return (dp, e, zs[dz % NZ] * NY + ys[dy % NY], mp)

    def plane(d):
        return zs[d % NZ]

    sibling, across, pair = (dp, 1 - e, f, mp), (1 - dp, e, f, mp), (dp, e, f, 1 - mp)

    off_s, off_k = pl.multiple_of((1 - dp) * half, half), pl.multiple_of(dp * half, half)
    at_s, at_k = pl.ds(GATE, half), pl.ds(GATE + half, half)
    own = rows.at[e, z, y]
    loads = [
        pltpu.make_async_copy(tok_hbm.at[:, pl.ds(off_s, half)], own.at[:, at_s], in_sem.at[0]),
        pltpu.make_async_copy(tok_hbm.at[:, pl.ds(off_k, half)], own.at[:, at_k], in_sem.at[1]),
        pltpu.make_async_copy(gate_hbm, gate_ref, in_sem.at[2]),
        pltpu.make_async_copy(route_hbm, route_ref, in_sem.at[3]),
    ]
    later = [
        pltpu.make_async_copy(hid_hbm, hid, in_sem.at[4]),
        pltpu.make_async_copy(w_hbm.at[:, pl.ds(off_s, half)], w.at[:, pl.ds(0, half)], in_sem.at[5]),
        pltpu.make_async_copy(w_hbm.at[:, pl.ds(off_k, half)], w.at[:, pl.ds(half, half)], in_sem.at[6]),
    ]
    for load in loads:
        load.start()
    barrier = pltpu.get_barrier_semaphore()
    around = [dev(dy=k) for k in YS] + [dev(dz=d) for d in ALL]
    partners = [sibling, across, pair, *around]
    for p in partners:
        pl.semaphore_signal(barrier, inc=1, device_id=p, device_id_type=MESH)
    for load in later:
        load.start()

    tok = rows.shape[3]
    diag = lax.broadcasted_iota(jnp.int32, (tok, tok), 0) == lax.broadcasted_iota(jnp.int32, (tok, tok), 1)
    lane = lax.broadcasted_iota(jnp.int32, (tok, GATE), 1)
    block = jnp.zeros((tok, GATE), jnp.float32)
    loads[2].wait()
    loads[3].wait()
    for expert in range(2):
        mine = jnp.sum(jnp.where(route_ref[...] == expert, gate_ref[...], 0.0), axis=0, keepdims=True)
        col = jnp.sum(jnp.where(diag, jnp.broadcast_to(mine, (tok, tok)), 0.0), axis=1, keepdims=True)
        high = col.astype(jnp.bfloat16).astype(jnp.float32)
        block = jnp.where(lane == 2 * expert, high, jnp.where(lane == 2 * expert + 1, col - high, block))
    rows[e, z, y, :, pl.ds(0, GATE)] = block.astype(jnp.bfloat16)
    loads[0].wait()
    loads[1].wait()
    numbers = {}

    def copy(key, src, dst, to):
        i = numbers.setdefault(key, len(numbers))
        return pltpu.make_async_remote_copy(
            src_ref=src, dst_ref=dst, send_sem=send_sem.at[i], recv_sem=recv_sem.at[i], device_id=to, device_id_type=MESH
        )

    def send(key, src, dst, to):
        c = copy(key, src, dst, to)
        c.start()
        sent.append(c)
        return c

    def wait(copies):
        for c in copies:
            c.wait_recv()

    spans = (pl.ds(0, GATE + half), pl.ds(GATE + half, half))

    class Gather:
        def __init__(self, core, n):
            self.n, self.reach = n, REACH[core][n]
            at = spans[n]
            self.a, self.b = pl.ds(at.start, SPLITS[n]), pl.ds(at.start + SPLITS[n], at.size - SPLITS[n])

        def a_plane(self, d, dz):
            ref = rows.at[e, plane(d), :, :, self.a]
            return send(("a_z", self.n, (d - dz) % NZ), ref, ref, dev(dz=dz))

        def b_block(self, d, dy=0, dz=0):
            ref = rows.at[e, plane(d), y, :, self.b]
            key = ("b_y", self.n, d % NZ, dy) if dy else ("b_z", self.n, (d - dz) % NZ)
            return send(key, ref, ref, dev(dy=dy, dz=dz))

        def spread(self, d):
            self.b_y[d % NZ] = [self.b_block(d, dy=k) for k in YS]

        def start(self):
            ref = rows.at[e, z, y, :, self.a]
            self.a_y = [send(("a_y", self.n, k), ref, ref, dev(dy=k)) for k in YS]
            self.b_z = {-dz % NZ: self.b_block(0, dz=dz) for dz in self.reach}
            self.b_y = {}
            self.spread(0)

        def a_near(self):
            wait(self.a_y)
            self.a_z = {-dz % NZ: self.a_plane(0, dz) for dz in self.reach}

        def b_near(self):
            for dz in self.reach:
                self.b_z[-dz % NZ].wait_recv()
                if len(self.reach) < NZ - 1:
                    if dz == 2:
                        self.b_z[5] = self.b_block(-2, dz=1)
                    if dz == -2:
                        self.b_z[3] = self.b_block(2, dz=-1)
                        self.b_z[4] = self.b_block(2, dz=-2)
                self.spread(-dz)

        def a_far(self):
            self.a_z[6].wait_recv()
            self.a_z[5] = self.a_plane(-2, 1)
            self.a_z[4] = self.a_plane(-2, 2)
            self.a_z[2].wait_recv()
            self.a_z[3] = self.a_plane(2, -1)

        def b_far(self):
            for d in (-3, 3, 4):
                self.b_z[d % NZ].wait_recv()
                self.spread(d)

        def shared(self, part, d):
            ref = rows.at[e, plane(d), :, :, self.a if part == "a" else self.b]
            return ("share", part, self.n, d), ref, ref, sibling

        def share(self, ds):
            for d in ds:
                if d and not (d in (2, -2) and len(self.reach) < NZ - 1):
                    self.a_z[d % NZ].wait_recv()
                send(*self.shared("a", d))
                wait(self.b_y[d % NZ])
                send(*self.shared("b", d))

        def receive(self, ds):
            for d in ds:
                for part in "ab":
                    copy(*self.shared(part, d)).wait_recv()

    n_rows = NY * tok

    def take(ds, at):
        parts = [rows[c, plane(d), :, :, at].reshape(n_rows, -1) for c in (mp, 1 - mp) for d in ds]
        return jnp.concatenate(parts, axis=0)

    def gate_of(ds):
        gates = take(ds, pl.ds(0, GATE)).astype(jnp.float32)
        lanes = lax.broadcasted_iota(jnp.int32, gates.shape, 1)
        return jnp.sum(jnp.where((lanes // 2) == e, gates, 0.0), axis=1, keepdims=True)

    def grow(i, ds, acc, start, n):
        x = take(ds, pl.ds(start + n, STEP))
        more = lax.dot_general(scaled[i], x, (((0,), (0,)), ((), ())), preferred_element_type=jnp.float32)
        return acc[:, n:n + STEP] + more if i else more

    def compute_s(i):
        ds = PAIRS[i]
        h = jnp.concatenate([hid[c, plane(d)] for c in (mp, 1 - mp) for d in ds], axis=0)
        scaled[i] = (h.astype(jnp.float32) * gate_of(ds)).astype(jnp.bfloat16)
        for n in range(0, half, STEP):
            total = grow(i, ds, acc_s, GATE, n)
            if i == len(PAIRS) - 1:
                at = pl.ds(n, STEP)
                gw_send[:, n:n + STEP] = total.astype(jnp.bfloat16)
                gw_sends.append(send(("gw", n), gw_send.at[:, at], gw_got.at[:, at], across))
            else:
                acc_s[:, n:n + STEP] = total

    def compute_k(i):
        ds = PAIRS[i]
        x = take(ds, pl.ds(GATE, width))
        gh = lax.dot_general(x, w[...], (((1,), (1,)), ((), ())), preferred_element_type=jnp.float32) * gate_of(ds)
        for j, d in enumerate(ds):
            gh_send[plane(d)] = gh[(j + 2) * n_rows:(j + 3) * n_rows].astype(jnp.bfloat16)
            gh_sends.append(send(("gh", d), gh_send.at[plane(d)], gh_got.at[plane(d)], pair))
            gh_keep[plane(d)] = gh[j * n_rows:(j + 1) * n_rows]
        for n in range(0, half, STEP):
            acc_k[:, n:n + STEP] = grow(i, ds, acc_k, GATE + half, n)

    def follow(order):
        loaded = {"s": later[:1], "k": later[1:]}
        for step, *args in order:
            if step in loaded:
                for load in loaded.pop(step):
                    load.wait()
            if step in "sk":
                (compute_s if step == "s" else compute_k)(*args)
            else:
                getattr(gathers[args[0]], step)(*args[1:])
        for c in sent:
            c.wait_send()
        wait(gh_sends)
        wait(gw_sends)

    pl.semaphore_wait(barrier, len(partners))
    for core, order in enumerate(ORDERS):
        gathers = [Gather(core, n) for n in range(2)]
        sent, gh_sends, gw_sends = [], [], []
        pl.when(e == core)(functools.partial(follow, order))


def finish(acc_k, gw_got, gh_keep, gh_got, gh_hbm, gw_hbm, gh, gw, sem):
    gh[...] = (gh_keep[...] + gh_got[...].astype(jnp.float32)).astype(jnp.bfloat16)
    outs = [pltpu.make_async_copy(gh, gh_hbm, sem.at[0])]
    outs[0].start()
    n = gw.shape[0] // 4
    for i in range(4):
        at = pl.ds(i * n, n)
        gw[at] = acc_k[at] + gw_got[at].astype(jnp.float32)
        outs.append(pltpu.make_async_copy(gw.at[at], gw_hbm.at[at], sem.at[i + 1]))
        outs[-1].start()
    for out in outs:
        out.wait()


def body(grad_tokens, routes, gates, hidden_act, weight):
    _, tok, width = grad_tokens.shape
    cap, ff = hidden_act.shape[2:]
    half, n_rows = width // 2, NY * tok
    vmem, hbm = pl.BlockSpec(memory_space=pltpu.VMEM), pl.BlockSpec(memory_space=pltpu.HBM)
    bf16, f32 = jnp.bfloat16, jnp.float32
    operands = (
        grad_tokens[0],
        gates[0].T,
        routes[0].T,
        hidden_act.reshape(2, NZ, n_rows, ff),
        weight[0],
    )
    halves = pl.pallas_call(
        kernel,
        out_shape=(
            pltpu.VMEM((ff, half), f32),
            pltpu.VMEM((ff, half), bf16),
            pltpu.VMEM((NZ, n_rows, ff), f32),
            pltpu.VMEM((NZ, n_rows, ff), bf16),
        ),
        in_specs=[hbm] * 5,
        out_specs=(vmem,) * 4,
        scratch_shapes=[
            pltpu.VMEM((2, tok), f32),
            pltpu.VMEM((2, tok), jnp.int32),
            pltpu.VMEM((2, NZ, NY, tok, GATE + width), bf16),
            pltpu.VMEM((2, NZ, n_rows, ff), bf16),
            pltpu.VMEM((len(PAIRS), 4 * n_rows, ff), bf16),
            pltpu.VMEM((ff, width), bf16),
            pltpu.VMEM((ff, half), f32),
            pltpu.VMEM((NZ, n_rows, ff), bf16),
            pltpu.VMEM((ff, half), bf16),
            pltpu.SemaphoreType.DMA((7,)),
            pltpu.SemaphoreType.DMA((N_COPIES,)),
            pltpu.SemaphoreType.DMA((N_COPIES,)),
        ],
        compiler_params=pltpu.CompilerParams(collective_id=0, has_side_effects=True, vmem_limit_bytes=32 * 2**20),
    )(*(pltpu.with_memory_space_constraint(x, pltpu.HBM) for x in operands))
    gh, gw = pl.pallas_call(
        finish,
        out_shape=(jax.ShapeDtypeStruct((NZ, n_rows, ff), bf16), jax.ShapeDtypeStruct((ff, half), f32)),
        in_specs=[vmem] * 4,
        out_specs=(hbm, hbm),
        scratch_shapes=[
            pltpu.VMEM((NZ, n_rows, ff), bf16),
            pltpu.VMEM((ff, half), f32),
            pltpu.SemaphoreType.DMA((5,)),
        ],
        compiler_params=pltpu.CompilerParams(vmem_limit_bytes=16 * 2**20),
    )(*halves)
    return gh.reshape(1, 1, cap // 2, ff), gw.reshape(1, ff, half)


def solution(mesh):
    in_specs = (
        P("dp", ("expert", "ff"), "mp"),
        P("dp", ("expert", "ff"), None),
        P("dp", ("expert", "ff"), None),
        P("dp", "expert", None, "ff"),
        P("expert", "ff", "mp"),
    )
    out_specs = (P("dp", "expert", "mp", "ff"), P("expert", "ff", ("mp", "dp")))
    return jax.shard_map(body, mesh=mesh, in_specs=in_specs, out_specs=out_specs, check_vma=False)
```

```python
import functools

import jax
import jax.numpy as jnp
from jax import lax
from jax.experimental import pallas as pl
from jax.experimental.pallas import tpu as pltpu
from jax.sharding import PartitionSpec as P

MESH = pl.DeviceIdType.MESH
NY, NZ = 4, 8
GATE = 128
SPLITS = (256, 256)
YS = (1, 3, 2)
NEAR = (2, -2, 1, -1)
ALL = (2, -2, 1, -1, 3, -3, 4)
REACH = ((ALL, ALL), (ALL, NEAR))
GROUPS = ((0,), (1, -1), (2, -2), (3, -3, 4))
STEP = 256
N_COPIES = 2 * (3 + 7 + 7 + 3 * NZ + 2 * NZ) + NZ + 4


ORDERS = ((
    ("start", 0),
    ("y_start", 1),
    ("a_near", 0),
    ("b_near", 0),
    ("share", 0, "a", (0,)),
    ("share", 0, "b", (0,)),
    ("z_start", 1),
    ("share", 1, "a", (0,)),
    ("share", 1, "b", (0,)),
    ("share", 0, "a", (-2,)),
    ("share", 0, "b", (-2,)),
    ("share", 0, "a", (2,)),
    ("share", 0, "b", (2,)),
    ("share", 0, "a", (-1,)),
    ("share", 0, "b", (-1,)),
    ("share", 0, "a", (1,)),
    ("share", 0, "b", (1,)),
    ("receive", 0, "ab", GROUPS[0]),
    ("s", 0, "ab"),
    ("receive", 1, "ab", GROUPS[0]),
    ("k", 0),
    ("share", 0, "a", (-3,)),
    ("share", 0, "b", (-3,)),
    ("share", 0, "a", (3,)),
    ("share", 0, "b", (3,)),
    ("share", 0, "a", (4,)),
    ("share", 0, "b", (4,)),
    ("a_near", 1),
    ("b_near", 1),
    ("receive", 0, "ab", GROUPS[1]),
    ("s", 1, "ab"),
    ("receive", 0, "ab", GROUPS[2]),
    ("s", 2, "ab"),
    ("receive", 0, "ab", GROUPS[3]),
    ("s", 3, "ab"),
    ("share", 1, "a", (-2,)),
    ("share", 1, "b", (-2,)),
    ("share", 1, "a", (2,)),
    ("share", 1, "b", (2,)),
    ("share", 1, "a", (-1,)),
    ("share", 1, "b", (-1,)),
    ("share", 1, "a", (1,)),
    ("share", 1, "b", (1,)),
    ("receive", 1, "ab", GROUPS[1]),
    ("k", 1),
    ("receive", 1, "ab", GROUPS[2]),
    ("k", 2),
    ("share", 1, "a", (-3,)),
    ("share", 1, "b", (-3,)),
    ("share", 1, "a", (3,)),
    ("share", 1, "b", (3,)),
    ("share", 1, "a", (4,)),
    ("share", 1, "b", (4,)),
    ("receive", 1, "ab", GROUPS[3]),
    ("k", 3),
), (
    ("start", 0),
    ("y_start", 1),
    ("a_near", 0),
    ("b_near", 0),
    ("share", 0, "a", (0,)),
    ("share", 0, "b", (0,)),
    ("z_start", 1),
    ("share", 1, "a", (0,)),
    ("share", 1, "b", (0,)),
    ("share", 0, "a", (-2,)),
    ("share", 0, "b", (-2,)),
    ("share", 0, "a", (2,)),
    ("share", 0, "b", (2,)),
    ("share", 0, "a", (-1,)),
    ("share", 0, "b", (-1,)),
    ("share", 0, "a", (1,)),
    ("share", 0, "b", (1,)),
    ("receive", 0, "ab", GROUPS[0]),
    ("s", 0, "ab"),
    ("receive", 1, "ab", GROUPS[0]),
    ("k", 0),
    ("share", 0, "a", (-3,)),
    ("share", 0, "b", (-3,)),
    ("share", 0, "a", (3,)),
    ("share", 0, "b", (3,)),
    ("share", 0, "a", (4,)),
    ("share", 0, "b", (4,)),
    ("a_near", 1),
    ("b_near", 1),
    ("receive", 0, "ab", GROUPS[1]),
    ("s", 1, "ab"),
    ("receive", 0, "ab", GROUPS[2]),
    ("s", 2, "ab"),
    ("receive", 0, "ab", GROUPS[3]),
    ("s", 3, "ab"),
    ("a_far", 1),
    ("b_far", 1),
    ("share", 1, "a", (-2,)),
    ("share", 1, "b", (-2,)),
    ("share", 1, "a", (2,)),
    ("share", 1, "b", (2,)),
    ("share", 1, "a", (-1,)),
    ("share", 1, "b", (-1,)),
    ("share", 1, "a", (1,)),
    ("share", 1, "b", (1,)),
    ("receive", 1, "ab", GROUPS[1]),
    ("k", 1),
    ("receive", 1, "ab", GROUPS[2]),
    ("k", 2),
    ("share", 1, "a", (-3,)),
    ("share", 1, "b", (-3,)),
    ("share", 1, "a", (3,)),
    ("share", 1, "b", (3,)),
    ("share", 1, "a", (4,)),
    ("share", 1, "b", (4,)),
    ("receive", 1, "ab", GROUPS[3]),
    ("k", 3),
))


def kernel(tok_hbm, gate_hbm, route_hbm, hid_hbm, w_hbm, acc_k, gw_got, gh_keep, gh_got,
           gate_ref, route_ref, rows, hid, scaled, w, acc_s, gh_send, gw_send, in_sem, send_sem, recv_sem):
    dp, e, f, mp = (lax.axis_index(a) for a in ("dp", "expert", "ff", "mp"))
    y, z = f & (NY - 1), f // NY
    ys, zs = [(y + k) & (NY - 1) for k in range(NY)], [(z + k) & (NZ - 1) for k in range(NZ)]
    width = w.shape[1]
    half = width // 2

    def dev(dy=0, dz=0):
        return (dp, e, zs[dz % NZ] * NY + ys[dy % NY], mp)

    def plane(d):
        return zs[d % NZ]

    sibling, across, pair = (dp, 1 - e, f, mp), (1 - dp, e, f, mp), (dp, e, f, 1 - mp)

    off_s, off_k = pl.multiple_of((1 - dp) * half, half), pl.multiple_of(dp * half, half)
    at_s, at_k = pl.ds(GATE, half), pl.ds(GATE + half, half)
    own = rows.at[e, z, y]
    loads = [
        pltpu.make_async_copy(tok_hbm.at[:, pl.ds(off_s, half)], own.at[:, at_s], in_sem.at[0]),
        pltpu.make_async_copy(tok_hbm.at[:, pl.ds(off_k, half)], own.at[:, at_k], in_sem.at[1]),
        pltpu.make_async_copy(gate_hbm, gate_ref, in_sem.at[2]),
        pltpu.make_async_copy(route_hbm, route_ref, in_sem.at[3]),
    ]
    later = [
        pltpu.make_async_copy(hid_hbm, hid, in_sem.at[4]),
        pltpu.make_async_copy(w_hbm.at[:, pl.ds(off_s, half)], w.at[:, pl.ds(0, half)], in_sem.at[5]),
        pltpu.make_async_copy(w_hbm.at[:, pl.ds(off_k, half)], w.at[:, pl.ds(half, half)], in_sem.at[6]),
    ]
    for load in loads:
        load.start()
    barrier = pltpu.get_barrier_semaphore()
    around = [dev(dy=k) for k in YS] + [dev(dz=d) for d in ALL]
    partners = [sibling, across, pair, *around]
    for p in partners:
        pl.semaphore_signal(barrier, inc=1, device_id=p, device_id_type=MESH)
    for load in later:
        load.start()

    tok = rows.shape[3]
    diag = lax.broadcasted_iota(jnp.int32, (tok, tok), 0) == lax.broadcasted_iota(jnp.int32, (tok, tok), 1)
    lane = lax.broadcasted_iota(jnp.int32, (tok, GATE), 1)
    block = jnp.zeros((tok, GATE), jnp.float32)
    loads[2].wait()
    loads[3].wait()
    for expert in range(2):
        mine = jnp.sum(jnp.where(route_ref[...] == expert, gate_ref[...], 0.0), axis=0, keepdims=True)
        col = jnp.sum(jnp.where(diag, jnp.broadcast_to(mine, (tok, tok)), 0.0), axis=1, keepdims=True)
        high = col.astype(jnp.bfloat16).astype(jnp.float32)
        block = jnp.where(lane == 2 * expert, high, jnp.where(lane == 2 * expert + 1, col - high, block))
    rows[e, z, y, :, pl.ds(0, GATE)] = block.astype(jnp.bfloat16)
    loads[0].wait()
    loads[1].wait()
    numbers = {}

    def copy(key, src, dst, to):
        i = numbers.setdefault(key, len(numbers))
        return pltpu.make_async_remote_copy(
            src_ref=src, dst_ref=dst, send_sem=send_sem.at[i], recv_sem=recv_sem.at[i], device_id=to, device_id_type=MESH
        )

    def send(key, src, dst, to):
        c = copy(key, src, dst, to)
        c.start()
        sent.append(c)
        return c

    def wait(copies):
        for c in copies:
            c.wait_recv()

    spans = (pl.ds(0, GATE + half), pl.ds(GATE + half, half))

    class Gather:
        def __init__(self, core, n):
            self.n, self.reach, self.b_y = n, REACH[core][n], {}
            at = spans[n]
            self.a, self.b = pl.ds(at.start, SPLITS[n]), pl.ds(at.start + SPLITS[n], at.size - SPLITS[n])

        def a_plane(self, d, dz):
            ref = rows.at[e, plane(d), :, :, self.a]
            return send(("a_z", self.n, (d - dz) % NZ), ref, ref, dev(dz=dz))

        def b_block(self, d, dy=0, dz=0):
            ref = rows.at[e, plane(d), y, :, self.b]
            key = ("b_y", self.n, d % NZ, dy) if dy else ("b_z", self.n, (d - dz) % NZ)
            return send(key, ref, ref, dev(dy=dy, dz=dz))

        def spread(self, d):
            self.b_y[d % NZ] = [self.b_block(d, dy=k) for k in YS]

        def start(self):
            ref = rows.at[e, z, y, :, self.a]
            self.a_y = [send(("a_y", self.n, k), ref, ref, dev(dy=k)) for k in YS]
            self.z_start()
            self.spread(0)

        def y_start(self):
            ref = rows.at[e, z, y, :, self.a]
            self.a_y = [send(("a_y", self.n, k), ref, ref, dev(dy=k)) for k in YS]
            self.spread(0)

        def z_start(self):
            self.b_z = {-dz % NZ: self.b_block(0, dz=dz) for dz in self.reach}

        def own_plane(self):
            wait(self.a_y)
            self.a_y = []

        def a_near(self):
            self.own_plane()
            self.a_z = {-dz % NZ: self.a_plane(0, dz) for dz in self.reach}

        def b_near(self):
            for dz in self.reach:
                self.b_z[-dz % NZ].wait_recv()
                if len(self.reach) < NZ - 1:
                    if dz == 2:
                        self.b_z[5] = self.b_block(-2, dz=1)
                    if dz == -2:
                        self.b_z[3] = self.b_block(2, dz=-1)
                        self.b_z[4] = self.b_block(2, dz=-2)
                self.spread(-dz)

        def a_far(self):
            self.a_z[6].wait_recv()
            self.a_z[5] = self.a_plane(-2, 1)
            self.a_z[4] = self.a_plane(-2, 2)
            self.a_z[2].wait_recv()
            self.a_z[3] = self.a_plane(2, -1)

        def b_far(self):
            for d in (-3, 3, 4):
                self.b_z[d % NZ].wait_recv()
                self.spread(d)

        def shared(self, part, d):
            ref = rows.at[e, plane(d), :, :, self.a if part == "a" else self.b]
            return ("share", part, self.n, d), ref, ref, sibling

        def share(self, part, ds):
            for d in ds:
                if part == "b":
                    wait(self.b_y[d % NZ])
                elif d == 0:
                    self.own_plane()
                elif d and not (d in (2, -2) and len(self.reach) < NZ - 1):
                    self.a_z[d % NZ].wait_recv()
                send(*self.shared(part, d))

        def receive(self, parts, ds):
            for d in ds:
                for part in parts:
                    copy(*self.shared(part, d)).wait_recv()

    n_rows = NY * tok

    def take(ds, at):
        parts = [rows[c, plane(d), :, :, at].reshape(n_rows, -1) for c in (mp, 1 - mp) for d in ds]
        return jnp.concatenate(parts, axis=0)

    def gate_of(ds):
        gates = take(ds, pl.ds(0, GATE)).astype(jnp.float32)
        lanes = lax.broadcasted_iota(jnp.int32, gates.shape, 1)
        return jnp.sum(jnp.where((lanes // 2) == e, gates, 0.0), axis=1, keepdims=True)

    def grow(i, ds, acc, start, at):
        h = jnp.concatenate([scaled[plane(d), j] for j in range(2) for d in ds], axis=0)
        x = take(ds, pl.ds(start + at.start, at.size))
        more = lax.dot_general(h, x, (((0,), (0,)), ((), ())), preferred_element_type=jnp.float32)
        return acc[:, at] + more if i else more

    def scale(i):
        ds = GROUPS[i]
        h = jnp.concatenate([hid[c, plane(d)] for c in (mp, 1 - mp) for d in ds], axis=0)
        h = (h.astype(jnp.float32) * gate_of(ds)).astype(jnp.bfloat16)
        for j in range(2):
            for k, d in enumerate(ds):
                at = (j * len(ds) + k) * n_rows
                scaled[plane(d), j] = h[at:at + n_rows]

    def compute_s(i, part):
        if part != "b":
            scale(i)
        first = SPLITS[0] - GATE
        start, stop = {"a": (0, first), "b": (first, half), "ab": (0, half)}[part]
        for n in range(start, stop, STEP):
            at = pl.ds(n, min(STEP, stop - n))
            total = grow(i, GROUPS[i], acc_s, GATE, at)
            if i == len(GROUPS) - 1:
                gw_send[:, at] = total.astype(jnp.bfloat16)
                gw_sends.append(send(("gw", n), gw_send.at[:, at], gw_got.at[:, at], across))
            else:
                acc_s[:, at] = total

    def compute_k(i):
        ds = GROUPS[i]
        x = take(ds, pl.ds(GATE, width))
        gh = lax.dot_general(x, w[...], (((1,), (1,)), ((), ())), preferred_element_type=jnp.float32) * gate_of(ds)
        for j, d in enumerate(ds):
            at = (j + len(ds)) * n_rows
            gh_send[plane(d)] = gh[at:at + n_rows].astype(jnp.bfloat16)
            gh_sends.append(send(("gh", d), gh_send.at[plane(d)], gh_got.at[plane(d)], pair))
            gh_keep[plane(d)] = gh[j * n_rows:(j + 1) * n_rows]
        for n in range(0, half, STEP):
            at = pl.ds(n, STEP)
            acc_k[:, at] = grow(i, ds, acc_k, GATE + half, at)

    def follow(order):
        loaded = {"s": later[:1], "k": later[1:]}
        for step, *args in order:
            if step in loaded:
                for load in loaded.pop(step):
                    load.wait()
            if step in "sk":
                (compute_s if step == "s" else compute_k)(*args)
            else:
                getattr(gathers[args[0]], step)(*args[1:])
        for c in sent:
            c.wait_send()
        wait(gh_sends)
        wait(gw_sends)

    pl.semaphore_wait(barrier, len(partners))
    for core, order in enumerate(ORDERS):
        gathers = [Gather(core, n) for n in range(2)]
        sent, gh_sends, gw_sends = [], [], []
        pl.when(e == core)(functools.partial(follow, order))


def finish(acc_k, gw_got, gh_keep, gh_got, gh_hbm, gw_hbm, gh, gw, sem):
    gh[...] = (gh_keep[...] + gh_got[...].astype(jnp.float32)).astype(jnp.bfloat16)
    outs = [pltpu.make_async_copy(gh, gh_hbm, sem.at[0])]
    outs[0].start()
    n = gw.shape[0] // 4
    for i in range(4):
        at = pl.ds(i * n, n)
        gw[at] = acc_k[at] + gw_got[at].astype(jnp.float32)
        outs.append(pltpu.make_async_copy(gw.at[at], gw_hbm.at[at], sem.at[i + 1]))
        outs[-1].start()
    for out in outs:
        out.wait()


def body(grad_tokens, routes, gates, hidden_act, weight):
    _, tok, width = grad_tokens.shape
    cap, ff = hidden_act.shape[2:]
    half, n_rows = width // 2, NY * tok
    vmem, hbm = pl.BlockSpec(memory_space=pltpu.VMEM), pl.BlockSpec(memory_space=pltpu.HBM)
    bf16, f32 = jnp.bfloat16, jnp.float32
    operands = (
        grad_tokens[0],
        gates[0].T,
        routes[0].T,
        hidden_act.reshape(2, NZ, n_rows, ff),
        weight[0],
    )
    halves = pl.pallas_call(
        kernel,
        out_shape=(
            pltpu.VMEM((ff, half), f32),
            pltpu.VMEM((ff, half), bf16),
            pltpu.VMEM((NZ, n_rows, ff), f32),
            pltpu.VMEM((NZ, n_rows, ff), bf16),
        ),
        in_specs=[hbm] * 5,
        out_specs=(vmem,) * 4,
        scratch_shapes=[
            pltpu.VMEM((2, tok), f32),
            pltpu.VMEM((2, tok), jnp.int32),
            pltpu.VMEM((2, NZ, NY, tok, GATE + width), bf16),
            pltpu.VMEM((2, NZ, n_rows, ff), bf16),
            pltpu.VMEM((NZ, 2, n_rows, ff), bf16),
            pltpu.VMEM((ff, width), bf16),
            pltpu.VMEM((ff, half), f32),
            pltpu.VMEM((NZ, n_rows, ff), bf16),
            pltpu.VMEM((ff, half), bf16),
            pltpu.SemaphoreType.DMA((7,)),
            pltpu.SemaphoreType.DMA((N_COPIES,)),
            pltpu.SemaphoreType.DMA((N_COPIES,)),
        ],
        compiler_params=pltpu.CompilerParams(collective_id=0, has_side_effects=True, vmem_limit_bytes=32 * 2**20),
    )(*(pltpu.with_memory_space_constraint(x, pltpu.HBM) for x in operands))
    gh, gw = pl.pallas_call(
        finish,
        out_shape=(jax.ShapeDtypeStruct((NZ, n_rows, ff), bf16), jax.ShapeDtypeStruct((ff, half), f32)),
        in_specs=[vmem] * 4,
        out_specs=(hbm, hbm),
        scratch_shapes=[
            pltpu.VMEM((NZ, n_rows, ff), bf16),
            pltpu.VMEM((ff, half), f32),
            pltpu.SemaphoreType.DMA((5,)),
        ],
        compiler_params=pltpu.CompilerParams(vmem_limit_bytes=16 * 2**20),
    )(*halves)
    return gh.reshape(1, 1, cap // 2, ff), gw.reshape(1, ff, half)


def solution(mesh):
    in_specs = (
        P("dp", ("expert", "ff"), "mp"),
        P("dp", ("expert", "ff"), None),
        P("dp", ("expert", "ff"), None),
        P("dp", "expert", None, "ff"),
        P("expert", "ff", "mp"),
    )
    out_specs = (P("dp", "expert", "mp", "ff"), P("expert", "ff", ("mp", "dp")))
    return jax.shard_map(body, mesh=mesh, in_specs=in_specs, out_specs=out_specs, check_vma=False)
```

```python
import functools

import jax
import jax.numpy as jnp
from jax import lax
from jax.experimental import pallas as pl
from jax.experimental.pallas import tpu as pltpu
from jax.sharding import PartitionSpec as P

MESH = pl.DeviceIdType.MESH
NY, NZ = 4, 8
GATE = 128
SPLITS = (256, 256)
YS = (1, 3, 2)
NEAR = (2, -2, 1, -1)
ALL = (2, -2, 1, -1, 3, -3, 4)
REACH = ((ALL, ALL), (ALL, NEAR))
GROUPS = ((0,), (1, -1), (2, -2), (3, -3, 4))
STEP = 256
N_COPIES = 2 * (3 + 7 + 7 + 3 * NZ + 2 * NZ) + NZ + 4


ORDERS = ((
    ("start", 0),
    ("y_start", 1),
    ("a_near", 0),
    ("b_near", 0),
    ("share", 0, "a", (0,)),
    ("share", 0, "b", (0,)),
    ("z_start", 1),
    ("share", 1, "a", (0,)),
    ("share", 1, "b", (0,)),
    ("share", 0, "a", (-2,)),
    ("share", 0, "b", (-2,)),
    ("share", 0, "a", (2,)),
    ("share", 0, "b", (2,)),
    ("share", 0, "a", (-1,)),
    ("share", 0, "b", (-1,)),
    ("share", 0, "a", (1,)),
    ("share", 0, "b", (1,)),
    ("receive", 0, "ab", GROUPS[0]),
    ("s", 0, "ab"),
    ("receive", 1, "ab", GROUPS[0]),
    ("k", 0),
    ("share", 0, "a", (-3,)),
    ("share", 0, "b", (-3,)),
    ("share", 0, "a", (3,)),
    ("share", 0, "b", (3,)),
    ("share", 0, "a", (4,)),
    ("share", 0, "b", (4,)),
    ("a_near", 1),
    ("b_near", 1),
    ("receive", 0, "ab", GROUPS[1]),
    ("s", 1, "ab"),
    ("receive", 0, "ab", GROUPS[2]),
    ("s", 2, "ab"),
    ("receive", 0, "ab", GROUPS[3]),
    ("s", 3, "ab"),
    ("share", 1, "a", (-2,)),
    ("share", 1, "b", (-2,)),
    ("share", 1, "a", (2,)),
    ("share", 1, "b", (2,)),
    ("share", 1, "a", (-1,)),
    ("share", 1, "b", (-1,)),
    ("share", 1, "a", (1,)),
    ("share", 1, "b", (1,)),
    ("receive", 1, "ab", GROUPS[1]),
    ("k", 1),
    ("receive", 1, "ab", GROUPS[2]),
    ("k", 2),
    ("share", 1, "a", (-3,)),
    ("share", 1, "b", (-3,)),
    ("share", 1, "a", (3,)),
    ("share", 1, "b", (3,)),
    ("share", 1, "a", (4,)),
    ("share", 1, "b", (4,)),
    ("receive", 1, "ab", GROUPS[3]),
    ("k", 3),
), (
    ("start", 0),
    ("y_start", 1),
    ("a_near", 0),
    ("b_near", 0),
    ("share", 0, "a", (0,)),
    ("share", 0, "b", (0,)),
    ("z_start", 1),
    ("share", 1, "a", (0,)),
    ("share", 1, "b", (0,)),
    ("share", 0, "a", (-2,)),
    ("share", 0, "b", (-2,)),
    ("share", 0, "a", (2,)),
    ("share", 0, "b", (2,)),
    ("share", 0, "a", (-1,)),
    ("share", 0, "b", (-1,)),
    ("share", 0, "a", (1,)),
    ("share", 0, "b", (1,)),
    ("receive", 0, "ab", GROUPS[0]),
    ("s", 0, "ab"),
    ("receive", 1, "ab", GROUPS[0]),
    ("k", 0),
    ("share", 0, "a", (-3,)),
    ("share", 0, "b", (-3,)),
    ("share", 0, "a", (3,)),
    ("share", 0, "b", (3,)),
    ("share", 0, "a", (4,)),
    ("share", 0, "b", (4,)),
    ("a_near", 1),
    ("b_near", 1),
    ("receive", 0, "ab", GROUPS[1]),
    ("s", 1, "ab"),
    ("receive", 0, "ab", GROUPS[2]),
    ("s", 2, "ab"),
    ("receive", 0, "ab", GROUPS[3]),
    ("s", 3, "ab"),
    ("a_far", 1),
    ("b_far", 1),
    ("share", 1, "a", (-2,)),
    ("share", 1, "b", (-2,)),
    ("share", 1, "a", (2,)),
    ("share", 1, "b", (2,)),
    ("share", 1, "a", (-1,)),
    ("share", 1, "b", (-1,)),
    ("share", 1, "a", (1,)),
    ("share", 1, "b", (1,)),
    ("receive", 1, "ab", GROUPS[1]),
    ("k", 1),
    ("receive", 1, "ab", GROUPS[2]),
    ("k", 2),
    ("share", 1, "a", (-3,)),
    ("share", 1, "b", (-3,)),
    ("share", 1, "a", (3,)),
    ("share", 1, "b", (3,)),
    ("share", 1, "a", (4,)),
    ("share", 1, "b", (4,)),
    ("receive", 1, "ab", GROUPS[3]),
    ("k", 3),
))


def kernel(tok_hbm, gate_hbm, route_hbm, hid_hbm, w_hbm, acc_k, gh_sum,
           gw_got, gh_keep, gh_got, gate_ref, route_ref, rows, hid, scaled, w, acc_s, gh_send, gw_send, in_sem, send_sem, recv_sem):
    dp, e, f, mp = (lax.axis_index(a) for a in ("dp", "expert", "ff", "mp"))
    y, z = f & (NY - 1), f // NY
    ys, zs = [(y + k) & (NY - 1) for k in range(NY)], [(z + k) & (NZ - 1) for k in range(NZ)]
    width = w.shape[1]
    half = width // 2

    def dev(dy=0, dz=0):
        return (dp, e, zs[dz % NZ] * NY + ys[dy % NY], mp)

    def plane(d):
        return zs[d % NZ]

    sibling, across, pair = (dp, 1 - e, f, mp), (1 - dp, e, f, mp), (dp, e, f, 1 - mp)

    off_s, off_k = pl.multiple_of((1 - dp) * half, half), pl.multiple_of(dp * half, half)
    at_s, at_k = pl.ds(GATE, half), pl.ds(GATE + half, half)
    own = rows.at[e, z, y]
    loads = [
        pltpu.make_async_copy(tok_hbm.at[:, pl.ds(off_s, half)], own.at[:, at_s], in_sem.at[0]),
        pltpu.make_async_copy(tok_hbm.at[:, pl.ds(off_k, half)], own.at[:, at_k], in_sem.at[1]),
        pltpu.make_async_copy(gate_hbm, gate_ref, in_sem.at[2]),
        pltpu.make_async_copy(route_hbm, route_ref, in_sem.at[3]),
    ]
    later = [
        pltpu.make_async_copy(hid_hbm, hid, in_sem.at[4]),
        pltpu.make_async_copy(w_hbm.at[:, pl.ds(off_s, half)], w.at[:, pl.ds(0, half)], in_sem.at[5]),
        pltpu.make_async_copy(w_hbm.at[:, pl.ds(off_k, half)], w.at[:, pl.ds(half, half)], in_sem.at[6]),
    ]
    for load in loads:
        load.start()
    barrier = pltpu.get_barrier_semaphore()
    around = [dev(dy=k) for k in YS] + [dev(dz=d) for d in ALL]
    partners = [sibling, across, pair, *around]
    for p in partners:
        pl.semaphore_signal(barrier, inc=1, device_id=p, device_id_type=MESH)
    for load in later:
        load.start()

    tok = rows.shape[3]
    diag = lax.broadcasted_iota(jnp.int32, (tok, tok), 0) == lax.broadcasted_iota(jnp.int32, (tok, tok), 1)
    lane = lax.broadcasted_iota(jnp.int32, (tok, GATE), 1)
    block = jnp.zeros((tok, GATE), jnp.float32)
    loads[2].wait()
    loads[3].wait()
    for expert in range(2):
        mine = jnp.sum(jnp.where(route_ref[...] == expert, gate_ref[...], 0.0), axis=0, keepdims=True)
        col = jnp.sum(jnp.where(diag, jnp.broadcast_to(mine, (tok, tok)), 0.0), axis=1, keepdims=True)
        high = col.astype(jnp.bfloat16).astype(jnp.float32)
        block = jnp.where(lane == 2 * expert, high, jnp.where(lane == 2 * expert + 1, col - high, block))
    rows[e, z, y, :, pl.ds(0, GATE)] = block.astype(jnp.bfloat16)
    loads[0].wait()
    loads[1].wait()
    numbers = {}

    def copy(key, src, dst, to):
        i = numbers.setdefault(key, len(numbers))
        return pltpu.make_async_remote_copy(
            src_ref=src, dst_ref=dst, send_sem=send_sem.at[i], recv_sem=recv_sem.at[i], device_id=to, device_id_type=MESH
        )

    def send(key, src, dst, to):
        c = copy(key, src, dst, to)
        c.start()
        sent.append(c)
        return c

    def wait(copies):
        for c in copies:
            c.wait_recv()

    spans = (pl.ds(0, GATE + half), pl.ds(GATE + half, half))

    class Gather:
        def __init__(self, core, n):
            self.n, self.reach, self.b_y = n, REACH[core][n], {}
            at = spans[n]
            self.a, self.b = pl.ds(at.start, SPLITS[n]), pl.ds(at.start + SPLITS[n], at.size - SPLITS[n])

        def a_plane(self, d, dz):
            ref = rows.at[e, plane(d), :, :, self.a]
            return send(("a_z", self.n, (d - dz) % NZ), ref, ref, dev(dz=dz))

        def b_block(self, d, dy=0, dz=0):
            ref = rows.at[e, plane(d), y, :, self.b]
            key = ("b_y", self.n, d % NZ, dy) if dy else ("b_z", self.n, (d - dz) % NZ)
            return send(key, ref, ref, dev(dy=dy, dz=dz))

        def spread(self, d):
            self.b_y[d % NZ] = [self.b_block(d, dy=k) for k in YS]

        def start(self):
            ref = rows.at[e, z, y, :, self.a]
            self.a_y = [send(("a_y", self.n, k), ref, ref, dev(dy=k)) for k in YS]
            self.z_start()
            self.spread(0)

        def y_start(self):
            ref = rows.at[e, z, y, :, self.a]
            self.a_y = [send(("a_y", self.n, k), ref, ref, dev(dy=k)) for k in YS]
            self.spread(0)

        def z_start(self):
            self.b_z = {-dz % NZ: self.b_block(0, dz=dz) for dz in self.reach}

        def own_plane(self):
            wait(self.a_y)
            self.a_y = []

        def a_near(self):
            self.own_plane()
            self.a_z = {-dz % NZ: self.a_plane(0, dz) for dz in self.reach}

        def b_near(self):
            for dz in self.reach:
                self.b_z[-dz % NZ].wait_recv()
                if len(self.reach) < NZ - 1:
                    if dz == 2:
                        self.b_z[5] = self.b_block(-2, dz=1)
                    if dz == -2:
                        self.b_z[3] = self.b_block(2, dz=-1)
                        self.b_z[4] = self.b_block(2, dz=-2)
                self.spread(-dz)

        def a_far(self):
            self.a_z[6].wait_recv()
            self.a_z[5] = self.a_plane(-2, 1)
            self.a_z[4] = self.a_plane(-2, 2)
            self.a_z[2].wait_recv()
            self.a_z[3] = self.a_plane(2, -1)

        def b_far(self):
            for d in (-3, 3, 4):
                self.b_z[d % NZ].wait_recv()
                self.spread(d)

        def shared(self, part, d):
            ref = rows.at[e, plane(d), :, :, self.a if part == "a" else self.b]
            return ("share", part, self.n, d), ref, ref, sibling

        def share(self, part, ds):
            for d in ds:
                if part == "b":
                    wait(self.b_y[d % NZ])
                elif d == 0:
                    self.own_plane()
                elif d and not (d in (2, -2) and len(self.reach) < NZ - 1):
                    self.a_z[d % NZ].wait_recv()
                send(*self.shared(part, d))

        def receive(self, parts, ds):
            for d in ds:
                for part in parts:
                    copy(*self.shared(part, d)).wait_recv()

    n_rows = NY * tok

    def take(ds, at):
        parts = [rows[c, plane(d), :, :, at].reshape(n_rows, -1) for c in (mp, 1 - mp) for d in ds]
        return jnp.concatenate(parts, axis=0)

    def gate_of(ds):
        gates = take(ds, pl.ds(0, GATE)).astype(jnp.float32)
        lanes = lax.broadcasted_iota(jnp.int32, gates.shape, 1)
        return jnp.sum(jnp.where((lanes // 2) == e, gates, 0.0), axis=1, keepdims=True)

    def grow(i, ds, acc, start, at):
        h = jnp.concatenate([scaled[plane(d), j] for j in range(2) for d in ds], axis=0)
        x = take(ds, pl.ds(start + at.start, at.size))
        more = lax.dot_general(h, x, (((0,), (0,)), ((), ())), preferred_element_type=jnp.float32)
        return acc[:, at] + more if i else more

    def scale(i):
        ds = GROUPS[i]
        h = jnp.concatenate([hid[c, plane(d)] for c in (mp, 1 - mp) for d in ds], axis=0)
        h = (h.astype(jnp.float32) * gate_of(ds)).astype(jnp.bfloat16)
        for j in range(2):
            for k, d in enumerate(ds):
                at = (j * len(ds) + k) * n_rows
                scaled[plane(d), j] = h[at:at + n_rows]

    def compute_s(i, part):
        if part != "b":
            scale(i)
        first = SPLITS[0] - GATE
        start, stop = {"a": (0, first), "b": (first, half), "ab": (0, half)}[part]
        for n in range(start, stop, STEP):
            at = pl.ds(n, min(STEP, stop - n))
            total = grow(i, GROUPS[i], acc_s, GATE, at)
            if i == len(GROUPS) - 1:
                gw_send[:, at] = total.astype(jnp.bfloat16)
                gw_sends.append(send(("gw", n), gw_send.at[:, at], gw_got.at[:, at], across))
            else:
                acc_s[:, at] = total

    def compute_k(i):
        ds = GROUPS[i]
        x = take(ds, pl.ds(GATE, width))
        gh = lax.dot_general(x, w[...], (((1,), (1,)), ((), ())), preferred_element_type=jnp.float32) * gate_of(ds)
        for j, d in enumerate(ds):
            at = (j + len(ds)) * n_rows
            gh_send[plane(d)] = gh[at:at + n_rows].astype(jnp.bfloat16)
            gh_sends.append(send(("gh", d), gh_send.at[plane(d)], gh_got.at[plane(d)], pair))
            gh_keep[plane(d)] = gh[j * n_rows:(j + 1) * n_rows]
        for n in range(0, half, STEP):
            at = pl.ds(n, STEP)
            acc_k[:, at] = grow(i, ds, acc_k, GATE + half, at)

    def follow(order):
        loaded = {"s": later[:1], "k": later[1:]}
        for step, *args in order:
            if step in loaded:
                for load in loaded.pop(step):
                    load.wait()
            if step in "sk":
                (compute_s if step == "s" else compute_k)(*args)
            else:
                getattr(gathers[args[0]], step)(*args[1:])
        for c in sent:
            c.wait_send()
        wait(gw_sends)
        acc_k[...] = acc_k[...] + gw_got[...].astype(jnp.float32)
        wait(gh_sends)
        gh_sum[...] = (gh_keep[...] + gh_got[...].astype(jnp.float32)).astype(jnp.bfloat16)

    pl.semaphore_wait(barrier, len(partners))
    for core, order in enumerate(ORDERS):
        gathers = [Gather(core, n) for n in range(2)]
        sent, gh_sends, gw_sends = [], [], []
        pl.when(e == core)(functools.partial(follow, order))


def store(gw, gh, gh_hbm, gw_hbm, sem):
    outs = [pltpu.make_async_copy(gw, gw_hbm, sem.at[0]), pltpu.make_async_copy(gh, gh_hbm, sem.at[1])]
    for out in outs:
        out.start()
    for out in outs:
        out.wait()


def body(grad_tokens, routes, gates, hidden_act, weight):
    _, tok, width = grad_tokens.shape
    cap, ff = hidden_act.shape[2:]
    half, n_rows = width // 2, NY * tok
    vmem, hbm = pl.BlockSpec(memory_space=pltpu.VMEM), pl.BlockSpec(memory_space=pltpu.HBM)
    bf16, f32 = jnp.bfloat16, jnp.float32
    operands = (
        grad_tokens[0],
        gates[0].T,
        routes[0].T,
        hidden_act.reshape(2, NZ, n_rows, ff),
        weight[0],
    )
    halves = pl.pallas_call(
        kernel,
        out_shape=(
            pltpu.VMEM((ff, half), f32),
            pltpu.VMEM((NZ, n_rows, ff), bf16),
        ),
        in_specs=[hbm] * 5,
        out_specs=(vmem,) * 2,
        scratch_shapes=[
            pltpu.VMEM((ff, half), bf16),
            pltpu.VMEM((NZ, n_rows, ff), f32),
            pltpu.VMEM((NZ, n_rows, ff), bf16),
            pltpu.VMEM((2, tok), f32),
            pltpu.VMEM((2, tok), jnp.int32),
            pltpu.VMEM((2, NZ, NY, tok, GATE + width), bf16),
            pltpu.VMEM((2, NZ, n_rows, ff), bf16),
            pltpu.VMEM((NZ, 2, n_rows, ff), bf16),
            pltpu.VMEM((ff, width), bf16),
            pltpu.VMEM((ff, half), f32),
            pltpu.VMEM((NZ, n_rows, ff), bf16),
            pltpu.VMEM((ff, half), bf16),
            pltpu.SemaphoreType.DMA((7,)),
            pltpu.SemaphoreType.DMA((N_COPIES,)),
            pltpu.SemaphoreType.DMA((N_COPIES,)),
        ],
        compiler_params=pltpu.CompilerParams(collective_id=0, has_side_effects=True, vmem_limit_bytes=32 * 2**20),
    )(*(pltpu.with_memory_space_constraint(x, pltpu.HBM) for x in operands))
    gh, gw = pl.pallas_call(
        store,
        out_shape=(jax.ShapeDtypeStruct((NZ, n_rows, ff), bf16), jax.ShapeDtypeStruct((ff, half), f32)),
        in_specs=[vmem] * 2,
        out_specs=(hbm, hbm),
        scratch_shapes=[pltpu.SemaphoreType.DMA((2,))],
        compiler_params=pltpu.CompilerParams(vmem_limit_bytes=16 * 2**20),
    )(*halves)
    return gh.reshape(1, 1, cap // 2, ff), gw.reshape(1, ff, half)


def solution(mesh):
    in_specs = (
        P("dp", ("expert", "ff"), "mp"),
        P("dp", ("expert", "ff"), None),
        P("dp", ("expert", "ff"), None),
        P("dp", "expert", None, "ff"),
        P("expert", "ff", "mp"),
    )
    out_specs = (P("dp", "expert", "mp", "ff"), P("expert", "ff", ("mp", "dp")))
    return jax.shard_map(body, mesh=mesh, in_specs=in_specs, out_specs=out_specs, check_vma=False)
```
